512 devices in a mesh: row: 32 (over z, x), inw: 8 (over y_lo, core), outw: 2 (over y_hi).
Axes of the slice: x: 4, y: 8 (y_hi: 2, y_lo: 4; y = y_hi * 4 + y_lo), z: 8, core: 2. Of those that a mesh axis runs over, the one named last changes fastest.
Arguments:
- inputs: bfloat16 [768, 8192], P('row', ('inw', 'outw')), may hold values from -6 to 6
- out_grad: bfloat16 [768, 8192], P('row', ('inw', 'outw')), may hold values from -3 to 3
- gate_weight: bfloat16 [8192, 16384], P(('inw', 'outw'), 'row'), may hold values from -0.0625 to 0.0625
- up_weight: bfloat16 [8192, 16384], P(('inw', 'outw'), 'row'), may hold values from -0.0625 to 0.0625
- down_weight: bfloat16 [16384, 8192], P('row', ('inw', 'outw')), may hold values from -0.046875 to 0.046875
Outputs:
- grad_inputs: bfloat16 [768, 8192], P('row', ('inw', 'outw'))
- grad_gate: bfloat16 [8192, 16384], P(('inw', 'outw'), 'row')
- grad_up: bfloat16 [8192, 16384], P(('inw', 'outw'), 'row')
- grad_down: bfloat16 [16384, 8192], P('row', ('inw', 'outw'))
The draws below stay inside these ranges and needn't reach their ends.
All inputs are finite; a program needn't handle non-finite values.
Results may differ from the reference program's by a relative error of at most 0.0049.
Values may be sent and summed in bfloat16 or wider, within the bound.
A program may use at most 64 MiB of HBM per device.

```python
import jax
import jax.numpy as jnp

D = 8192
F = 16384
TOKENS = 768


def block_levels(key, shape, pieces, least, largest):
    def one(axis_at, shards_of):
        draws = jax.random.uniform(jax.random.fold_in(jax.random.fold_in(key, 6), axis_at), (shards_of,), jnp.float32, least / len(pieces), largest / len(pieces))
        return jnp.repeat(jnp.exp(draws), shape[axis_at] // shards_of).reshape((-1,) + (1,) * (len(shape) - axis_at - 1))

    factor_of = one(*pieces[0])
    for cut in pieces[1:]:
        factor_of = factor_of * one(*cut)
    return factor_of


def gaussian(rng, shape, width, bound, pieces=(), dtype=jnp.bfloat16):
    drawn = jax.random.normal(rng, shape, jnp.float32) * width
    if len(pieces) > 0:
        drawn = block_levels(rng, shape, pieces, -0.22, 0.18) * drawn
    return jnp.clip(drawn, min=-bound, max=bound).astype(dtype)


def setup_inputs(seed: int = 0) -> dict:
    streams_of = jax.random.split(jax.random.key(seed), 6)
    return {
        "inputs": gaussian(streams_of[0], (TOKENS, D), 1.0, 6.0, ((0, 32), (1, 16))),
        "out_grad": gaussian(streams_of[1], (TOKENS, D), 0.5, 3.0, ((0, 32), (1, 16))),
        "gate_weight": gaussian(streams_of[2], (D, F), D ** -0.5, 0.0625, ((0, 16), (1, 32))),
        "up_weight": gaussian(streams_of[3], (D, F), D ** -0.5, 0.0625, ((0, 16), (1, 32))),
        "down_weight": gaussian(streams_of[4], (F, D), F ** -0.5, 0.046875, ((0, 32), (1, 16))),
    }


def reference(inputs, out_grad, gate_weight, up_weight, down_weight):
    gate = jnp.dot(inputs, gate_weight, preferred_element_type=jnp.float32)
    up = jnp.dot(inputs, up_weight, preferred_element_type=jnp.float32)
    back = jnp.dot(out_grad, down_weight.T, preferred_element_type=jnp.float32)
    sigmoid_gate = jax.nn.sigmoid(gate)
    silu_gate = gate * sigmoid_gate
    hidden = (silu_gate * up).astype(jnp.bfloat16)
    gate_grad = (back * up * sigmoid_gate * (1.0 + gate * (1.0 - sigmoid_gate))).astype(jnp.bfloat16)
    up_grad = (back * silu_gate).astype(jnp.bfloat16)
    grad_down = jnp.dot(hidden.T, out_grad, preferred_element_type=jnp.float32).astype(jnp.bfloat16)
    grad_gate = jnp.dot(inputs.T, gate_grad, preferred_element_type=jnp.float32).astype(jnp.bfloat16)
    grad_up = jnp.dot(inputs.T, up_grad, preferred_element_type=jnp.float32).astype(jnp.bfloat16)
    total = jnp.dot(gate_grad, gate_weight.T, preferred_element_type=jnp.float32)
    total = total + jnp.dot(up_grad, up_weight.T, preferred_element_type=jnp.float32)
    grad_inputs = total.astype(jnp.bfloat16)
    return grad_inputs, grad_gate, grad_up, grad_down
```

```python
import functools

import jax
import jax.numpy as jnp
from jax import lax
from jax.experimental import pallas as pl
from jax.experimental.pallas import tpu as pltpu
from jax.sharding import PartitionSpec as P

MESH = pl.DeviceIdType.MESH
BF, F32 = jnp.bfloat16, jnp.float32
NZ, NX, NY = 8, 4, 8
GROUPS = {0: ((0, 1), (2,)), 1: ((0, 1, 2),), 2: ((0, 1, 2),), 3: ((0, 1, 2),)}


def dot(a, b):
    return jnp.dot(a, b, preferred_element_type=F32)


def dot_nt(a, b):
    return lax.dot_general(a, b, (((1,), (1,)), ((), ())), preferred_element_type=F32)


def dot_tn(a, b):
    return lax.dot_general(a, b, (((0,), (0,)), ((), ())), preferred_element_type=F32)


def scratch(t, w, f):
    made = {
        "xb": ((NX, NZ, t, w), BF),
        "gb": ((NX, NZ, t, w), BF),
        "wg": ((2, w, f), BF),
        "wu": ((2, w, f), BF),
        "wd": ((2, f, w), BF),
        "hb": ((2, NX, NZ, 3, t, f), BF),
        "dxs": ((NX, NZ, t, w), F32),
        "dxr": ((NX, NZ, t, w), F32),
        "zs": ((NZ, t, w), BF),
        "zr": ((NZ, t, w), BF),
        "og": ((2, w, f), BF),
        "ou": ((2, w, f), BF),
        "od": ((2, f, w), BF),
    }
    for c, groups in GROUPS.items():
        for g, qs in enumerate(groups):
            n = len(qs)
            made[f"po{c}{g}"] = ((NZ, n, t, f), F32)
            made[f"cs{c}{g}"] = ((NZ, n, t, f), F32)
            made[f"cr{c}{g}"] = ((NZ, n, t, f), F32)
            made[f"pb{c}{g}"] = ((NZ, n, t, f), BF)
            made[f"rr{c}{g}"] = ((3, n, t, f), BF)
            made[f"sr{c}{g}"] = ((2, n, t, f), BF)
            made[f"ro{c}{g}"] = ((4, n, t, f), BF)
    return made


N_REMOTE = 160
N_LOCAL = 16


def kernel(names, x_ref, g_ref, wg_hbm, wu_hbm, wd_hbm, dx_ref, og_hbm, ou_hbm, od_hbm, *refs):
    buf = dict(zip(names, refs))
    ssem, rsem, lsem = refs[len(names) :]
    t, w = x_ref.shape
    f = wg_hbm.shape[1] // 2
    row, inw, outw = lax.axis_index("row"), lax.axis_index("inw"), lax.axis_index("outw")
    z, x = row // NX, row % NX
    y, core = outw * 4 + inw // 2, inw % 2
    s = 1 - 2 * core

    def dev(dz=0, dx=0, dy=0, other=False):
        zz, xx, yy = (z + dz + NZ) % NZ, (x + dx + NX) % NX, (y + dy + NY) % NY
        cc = 1 - core if other else core
        return (zz * NX + xx, (yy % 4) * 2 + cc, yy // 4)

    def at_y(k):
        return (y + k * s + NY) % NY

    def y_dev(k):
        return dev(dy=k * s)

    started, used = [], [0, 0]

    def send(src, dst, device):
        i = used[0]
        used[0] += 1
        copy = pltpu.make_async_remote_copy(
            src_ref=src, dst_ref=dst, send_sem=ssem.at[i], recv_sem=rsem.at[i], device_id=device, device_id_type=MESH
        )
        copy.start()
        started.append(copy)
        return copy

    def local(src, dst):
        i = used[1]
        used[1] += 1
        copy = pltpu.make_async_copy(src, dst, lsem.at[i])
        copy.start()
        return copy

    halves = [pl.ds(pl.multiple_of(h * f, f), f) for h in (core, 1 - core)]
    loads = []
    for h in range(2):
        loads.append(local(wg_hbm.at[:, halves[h]], buf["wg"].at[h]))
        loads.append(local(wu_hbm.at[:, halves[h]], buf["wu"].at[h]))
        loads.append(local(wd_hbm.at[halves[h], :], buf["wd"].at[h]))

    barrier = pltpu.get_barrier_semaphore()
    peers = [dev(dz=k) for k in range(1, NZ)] + [dev(dx=k) for k in range(1, NX)]
    peers += [dev(dy=k) for k in (1, -1, 2, -2)] + [dev(other=True)]
    for peer in peers:
        pl.semaphore_signal(barrier, inc=1, device_id=peer, device_id_type=MESH)
    xb, gb, hb = buf["xb"], buf["gb"], buf["hb"]
    xb[0, 0] = x_ref[...]
    gb[0, 0] = g_ref[...]
    pl.semaphore_wait(barrier, len(peers))

    got = {}
    near_first = (1, 7, 2, 6, 3, 5, 4)
    for k in near_first:
        got["zx", k] = send(x_ref, xb.at[0, k], dev(dz=k))
    for k in near_first:
        got["zg", k] = send(g_ref, gb.at[0, k], dev(dz=k))
    for copy in loads:
        copy.wait()

    def column(name, block):
        for k in near_first:
            got["z" + name, k].wait_recv()
        for c in (1, 3, 2):
            got["x" + name, c] = send(block.at[0], block.at[c], dev(dx=c))

    def products(c, g):
        for i, q in enumerate(GROUPS[c][g]):
            left = (gb if q == 2 else xb)[c].reshape(NZ * t, w)
            for h in (1, 0):
                if q == 2:
                    part = dot_nt(left, buf["wd"][h])
                else:
                    part = dot(left, buf["wu" if q else "wg"][h])
                to = buf[f"{'cs' if h else 'po'}{c}{g}"]
                to[:, i] = part.reshape(NZ, t, f)
        got["c", c, g] = send(buf[f"cs{c}{g}"], buf[f"cr{c}{g}"], dev(other=True))

    def arrive(c):
        got["xx", c].wait_recv()
        got["xg", c].wait_recv()

    def own(c, g, slot):
        return buf[f"po{c}{g}"][slot] + buf[f"cr{c}{g}"][slot]

    def leaf(c, g):
        got["c", c, g].wait_recv()
        pb, rr, ro = buf[f"pb{c}{g}"], buf[f"rr{c}{g}"], buf[f"ro{c}{g}"]
        for slot in range(NZ):
            pb[slot] = own(c, g, slot).astype(BF)
        got["l", c, g] = [
            send(pb.at[at_y(-3)], rr.at[0], y_dev(-1)),
            send(pb.at[at_y(-4)], rr.at[1], y_dev(-2)),
            send(pb.at[at_y(3)], rr.at[2], y_dev(1)),
        ]
        got["d", c, g] = [send(pb.at[at_y(-1)], ro.at[0], y_dev(-1)), send(pb.at[at_y(1)], ro.at[1], y_dev(1))]

    def relay(c, g):
        for copy in got["l", c, g]:
            copy.wait_recv()
        rr, sr, ro = buf[f"rr{c}{g}"], buf[f"sr{c}{g}"], buf[f"ro{c}{g}"]
        sr[0] = (own(c, g, at_y(-2)) + rr[0].astype(F32) + rr[1].astype(F32)).astype(BF)
        first = send(sr.at[0], ro.at[2], y_dev(-2))
        sr[1] = (own(c, g, at_y(2)) + rr[2].astype(F32)).astype(BF)
        got["d", c, g] += [first, send(sr.at[1], ro.at[3], y_dev(2))]

    def owner(c):
        sums = {}
        for g, qs in enumerate(GROUPS[c]):
            for copy in got["d", c, g]:
                copy.wait_recv()
            total = own(c, g, y)
            for i in range(4):
                total = total + buf[f"ro{c}{g}"][i].astype(F32)
            for i, q in enumerate(qs):
                sums[q] = total[i]
        gate, up, back = sums[0], sums[1], sums[2]
        sig = jax.nn.sigmoid(gate)
        silu = gate * sig
        hb[0, c, y, 0] = (back * up * sig * (1.0 + gate * (1.0 - sig))).astype(BF)
        hb[0, c, y, 1] = (back * silu).astype(BF)
        hb[0, c, y, 2] = (silu * up).astype(BF)

    def spread(c):
        mine = hb.at[0, c, y]
        for k in (2, -2, 1, -1):
            got["a", c, k] = send(mine, mine, y_dev(k))

    def pass_on(c):
        got["a", c, 2].wait_recv()
        block = hb.at[0, c, at_y(-2)]
        got["a", c, 4] = send(block, block, y_dev(2))
        got["a", c, 3] = send(block, block, y_dev(1))
        got["a", c, -2].wait_recv()
        block = hb.at[0, c, at_y(2)]
        got["a", c, -3] = send(block, block, y_dev(-1))

    def share(c):
        for k in (1, -1, 3, -3, 4):
            got["a", c, k].wait_recv()
        got["s", c] = send(hb.at[0, c], hb.at[1, c], dev(other=True))

    def back_product(c):
        got["s", c].wait_recv()
        total = None
        for h in range(2):
            for q, name in enumerate(("wg", "wu")):
                term = dot_nt(hb[h, c, :, q].reshape(NZ * t, f), buf[name][h])
                total = term if total is None else total + term
        buf["dxs"][c] = total.reshape(NZ, t, w)
        if c:
            got["dx", c] = send(buf["dxs"].at[c], buf["dxr"].at[c], dev(dx=-c))

    def reduce_inputs():
        for c in (1, 3, 2):
            got["dx", c].wait_recv()
        zs = buf["zs"]
        for k in (4, 3, 5, 2, 6, 1, 7):
            zs[k] = (buf["dxs"][0, k] + buf["dxr"][1, k] + buf["dxr"][2, k] + buf["dxr"][3, k]).astype(BF)
            got["zr", k] = send(zs.at[k], buf["zr"].at[k], dev(dz=-k))

    stores = []

    def weight_grads():
        left = xb[...].reshape(NX * NZ * t, w)
        for h in range(2):
            for q, name, out in ((0, "og", og_hbm), (1, "ou", ou_hbm)):
                right = hb[h, :, :, q].reshape(NX * NZ * t, f)
                buf[name][h] = dot_tn(left, right).astype(BF)
                stores.append(local(buf[name].at[h], out.at[:, halves[h]]))
        right = gb[...].reshape(NX * NZ * t, w)
        for h in range(2):
            left = hb[h, :, :, 2].reshape(NX * NZ * t, f)
            buf["od"][h] = dot_tn(left, right).astype(BF)
            stores.append(local(buf["od"].at[h], od_hbm.at[halves[h], :]))

    def finish():
        total = buf["dxs"][0, 0] + buf["dxr"][1, 0] + buf["dxr"][2, 0] + buf["dxr"][3, 0]
        for k in range(1, NZ):
            got["zr", k].wait_recv()
            total = total + buf["zr"][k].astype(F32)
        dx_ref[...] = total.astype(BF)

    column("x", xb)
    products(0, 0)
    leaf(0, 0)
    column("g", gb)
    products(0, 1)
    leaf(0, 1)
    relay(0, 0)
    relay(0, 1)
    arrive(1)
    products(1, 0)
    arrive(3)
    products(3, 0)
    owner(0)
    leaf(1, 0)
    leaf(3, 0)
    relay(1, 0)
    relay(3, 0)
    owner(1)
    spread(1)
    owner(3)
    spread(3)
    arrive(2)
    products(2, 0)
    leaf(2, 0)
    pass_on(1)
    pass_on(3)
    relay(2, 0)
    spread(0)
    share(1)
    share(3)
    back_product(1)
    owner(2)
    spread(2)
    back_product(3)
    pass_on(0)
    share(0)
    pass_on(2)
    back_product(0)
    share(2)
    back_product(2)
    reduce_inputs()
    weight_grads()
    finish()
    for copy in started:
        copy.wait_send()
    for copy in stores:
        copy.wait()


def per_device(inputs, out_grad, gate_weight, up_weight, down_weight):
    t, w = inputs.shape
    f = gate_weight.shape[1] // 2
    buffers = scratch(t, w, f)
    vmem, hbm = pl.BlockSpec(memory_space=pltpu.VMEM), pl.BlockSpec(memory_space=pl.ANY)
    flops = 2 * 8 * (NX * NZ * t) * w * (2 * f)
    return pl.pallas_call(
        functools.partial(kernel, list(buffers)),
        out_shape=(
            jax.ShapeDtypeStruct(inputs.shape, BF),
            jax.ShapeDtypeStruct(gate_weight.shape, BF),
            jax.ShapeDtypeStruct(up_weight.shape, BF),
            jax.ShapeDtypeStruct(down_weight.shape, BF),
        ),
        in_specs=[vmem, vmem, hbm, hbm, hbm],
        out_specs=(vmem, hbm, hbm, hbm),
        scratch_shapes=[pltpu.VMEM(shape, dtype) for shape, dtype in buffers.values()]
        + [
            pltpu.SemaphoreType.DMA((N_REMOTE,)),
            pltpu.SemaphoreType.DMA((N_REMOTE,)),
            pltpu.SemaphoreType.DMA((N_LOCAL,)),
        ],
        compiler_params=pltpu.CompilerParams(collective_id=0, has_side_effects=True, vmem_limit_bytes=56 << 20),
        cost_estimate=pl.CostEstimate(flops=flops, bytes_accessed=4 << 20, transcendentals=3 * NX * t * f),
    )(inputs, out_grad, gate_weight, up_weight, down_weight)


def solution(mesh):
    in_specs = (
        P("row", ("inw", "outw")),
        P("row", ("inw", "outw")),
        P(("inw", "outw"), "row"),
        P(("inw", "outw"), "row"),
        P("row", ("inw", "outw")),
    )
    out_specs = (
        P("row", ("inw", "outw")),
        P(("inw", "outw"), "row"),
        P(("inw", "outw"), "row"),
        P("row", ("inw", "outw")),
    )
    return jax.shard_map(per_device, mesh=mesh, in_specs=in_specs, out_specs=out_specs, check_vma=False)
```

```python
import functools

import jax
import jax.numpy as jnp
from jax import lax
from jax.experimental import pallas as pl
from jax.experimental.pallas import tpu as pltpu
from jax.sharding import PartitionSpec as P

MESH = pl.DeviceIdType.MESH
BF, F32 = jnp.bfloat16, jnp.float32
NZ, NX, NY = 8, 4, 8
GROUPS = {c: ((0, 1), (2,)) for c in range(NX)}


def dot(a, b):
    return jnp.dot(a, b, preferred_element_type=F32)


def dot_nt(a, b):
    return lax.dot_general(a, b, (((1,), (1,)), ((), ())), preferred_element_type=F32)


def dot_tn(a, b):
    return lax.dot_general(a, b, (((0,), (0,)), ((), ())), preferred_element_type=F32)


def scratch(t, w, f):
    made = {
        "xb": ((NX, NZ, t, w), BF),
        "gb": ((NX, NZ, t, w), BF),
        "wg": ((2, w, f), BF),
        "wu": ((2, w, f), BF),
        "wd": ((2, f, w), BF),
        "hb": ((2, NX, NZ, 2, t, f), BF),
        "hh": ((2, NY, NX, t, f), BF),
        "dx": ((NX, t, w), F32),
        "xr": ((NX, t, w), F32),
        "zs": ((NX, NZ, t, w), BF),
        "zr": ((NX, NZ, t, w), BF),
        "og": ((2, w, f), BF),
        "ou": ((2, w, f), BF),
        "od": ((2, f, w), BF),
    }
    for c, groups in GROUPS.items():
        for g, qs in enumerate(groups):
            n = len(qs)
            made[f"po{c}{g}"] = ((NZ, n, t, f), F32)
            made[f"cs{c}{g}"] = ((NZ, n, t, f), F32)
            made[f"cr{c}{g}"] = ((NZ, n, t, f), F32)
            made[f"pb{c}{g}"] = ((NZ, n, t, f), BF)
            made[f"rr{c}{g}"] = ((3, n, t, f), BF)
            made[f"sr{c}{g}"] = ((2, n, t, f), BF)
            made[f"ro{c}{g}"] = ((4, n, t, f), BF)
    return made


N_REMOTE = 256
N_LOCAL = 16


def kernel(names, x_ref, g_ref, wg_hbm, wu_hbm, wd_hbm, dx_ref, og_hbm, ou_hbm, od_hbm, *refs):
    buf = dict(zip(names, refs))
    ssem, rsem, lsem = refs[len(names) :]
    t, w = x_ref.shape
    f = wg_hbm.shape[1] // 2
    row, inw, outw = lax.axis_index("row"), lax.axis_index("inw"), lax.axis_index("outw")
    z, x = row // NX, row % NX
    y, core = outw * 4 + inw // 2, inw % 2
    s = 1 - 2 * core

    def dev(dz=0, dx=0, dy=0, other=False):
        zz, xx, yy = (z + dz + NZ) % NZ, (x + dx + NX) % NX, (y + dy + NY) % NY
        cc = 1 - core if other else core
        return (zz * NX + xx, (yy % 4) * 2 + cc, yy // 4)

    def at_y(k):
        return (y + k * s + NY) % NY

    def y_dev(k):
        return dev(dy=k * s)

    started, used = [], [0, 0]

    def send(src, dst, device):
        i = used[0]
        used[0] += 1
        copy = pltpu.make_async_remote_copy(
            src_ref=src, dst_ref=dst, send_sem=ssem.at[i], recv_sem=rsem.at[i], device_id=device, device_id_type=MESH
        )
        copy.start()
        started.append(copy)
        return copy

    def local(src, dst):
        i = used[1]
        used[1] += 1
        copy = pltpu.make_async_copy(src, dst, lsem.at[i])
        copy.start()
        return copy

    halves = [pl.ds(pl.multiple_of(h * f, f), f) for h in (core, 1 - core)]
    loads = []
    for h in range(2):
        loads.append(local(wg_hbm.at[:, halves[h]], buf["wg"].at[h]))
        loads.append(local(wu_hbm.at[:, halves[h]], buf["wu"].at[h]))
        loads.append(local(wd_hbm.at[halves[h], :], buf["wd"].at[h]))

    barrier = pltpu.get_barrier_semaphore()
    peers = [dev(dz=k) for k in range(1, NZ)] + [dev(dx=k) for k in range(1, NX)]
    peers += [dev(dy=k) for k in (1, -1, 2, -2)] + [dev(other=True)]
    for peer in peers:
        pl.semaphore_signal(barrier, inc=1, device_id=peer, device_id_type=MESH)
    xb, gb, hb, hh = buf["xb"], buf["gb"], buf["hb"], buf["hh"]
    xb[0, 0] = x_ref[...]
    gb[0, 0] = g_ref[...]
    pl.semaphore_wait(barrier, len(peers))

    got = {}
    stores = []
    blocks = {"x": (x_ref, xb), "g": (g_ref, gb)}

    def first(name, c):
        ref, block = blocks[name]
        got[name, c, 0] = send(ref, block.at[c, 0], dev(dx=c))

    def column(name):
        ref, block = blocks[name]
        for k in (1, 7, 2, 6, 3, 5, 4):
            got[name, 0, k] = send(ref, block.at[0, k], dev(dz=k))

    def forward(name, near):
        block = blocks[name][1]
        for k in (1, 7, 2, 6) if near else (3, 5, 4):
            got[name, 0, k].wait_recv()
        for start, size in ((1, 2), (6, 2)) if near else ((3, 3),):
            for c in (1, 3):
                part = pl.ds(start, size)
                got[name, c, start] = send(block.at[0, part], block.at[c, part], dev(dx=c))

    def across(name):
        block = blocks[name][1]
        got[name, 2, 0].wait_recv()
        for k in (1, 7, 2, 6, 3, 5, 4):
            got[name, 2, k] = send(block.at[2, 0], block.at[2, k], dev(dz=k))

    def arrive(c, name):
        for k in range(1, NZ) if c == 2 else (0, 1, 6, 3):
            got[name, c, k].wait_recv()

    def products(c, g):
        for i, q in enumerate(GROUPS[c][g]):
            left = (gb if q == 2 else xb)[c].reshape(NZ * t, w)
            for h in (1, 0):
                if q == 2:
                    part = dot_nt(left, buf["wd"][h])
                else:
                    part = dot(left, buf["wu" if q else "wg"][h])
                to = buf[f"{'cs' if h else 'po'}{c}{g}"]
                to[:, i] = part.reshape(NZ, t, f)
        got["c", c, g] = send(buf[f"cs{c}{g}"], buf[f"cr{c}{g}"], dev(other=True))

    def own(c, g, slot):
        return buf[f"po{c}{g}"][slot] + buf[f"cr{c}{g}"][slot]

    def leaf(c, g):
        got["c", c, g].wait_recv()
        pb, rr, ro = buf[f"pb{c}{g}"], buf[f"rr{c}{g}"], buf[f"ro{c}{g}"]
        for slot in range(NZ):
            pb[slot] = own(c, g, slot).astype(BF)
        got["l", c, g] = [
            send(pb.at[at_y(-3)], rr.at[0], y_dev(-1)),
            send(pb.at[at_y(-4)], rr.at[1], y_dev(-2)),
            send(pb.at[at_y(3)], rr.at[2], y_dev(1)),
        ]
        got["d", c, g] = [send(pb.at[at_y(-1)], ro.at[0], y_dev(-1)), send(pb.at[at_y(1)], ro.at[1], y_dev(1))]

    def relay(c, g):
        for copy in got["l", c, g]:
            copy.wait_recv()
        rr, sr, ro = buf[f"rr{c}{g}"], buf[f"sr{c}{g}"], buf[f"ro{c}{g}"]
        sr[0] = (own(c, g, at_y(-2)) + rr[0].astype(F32) + rr[1].astype(F32)).astype(BF)
        one = send(sr.at[0], ro.at[2], y_dev(-2))
        sr[1] = (own(c, g, at_y(2)) + rr[2].astype(F32)).astype(BF)
        got["d", c, g] += [one, send(sr.at[1], ro.at[3], y_dev(2))]

    def owner(c):
        sums = {}
        for g, qs in enumerate(GROUPS[c]):
            for copy in got["d", c, g]:
                copy.wait_recv()
            total = own(c, g, y)
            for i in range(4):
                total = total + buf[f"ro{c}{g}"][i].astype(F32)
            for i, q in enumerate(qs):
                sums[q] = total[i]
        gate, up, back = sums[0], sums[1], sums[2]
        sig = jax.nn.sigmoid(gate)
        silu = gate * sig
        hb[0, c, y, 0] = (back * up * sig * (1.0 + gate * (1.0 - sig))).astype(BF)
        hb[0, c, y, 1] = (back * silu).astype(BF)
        hh[0, y, c] = (silu * up).astype(BF)

    def result(c, slot):
        return hh.at[0, slot] if c == "h" else hb.at[0, c, slot]

    def spread(c):
        mine = result(c, y)
        for k in (2, -2, 1, -1):
            got["a", c, k] = send(mine, mine, y_dev(k))

    def pass_on(c):
        got["a", c, 2].wait_recv()
        block = result(c, at_y(-2))
        got["a", c, 4] = send(block, block, y_dev(2))
        got["a", c, 3] = send(block, block, y_dev(1))
        got["a", c, -2].wait_recv()
        block = result(c, at_y(2))
        got["a", c, -3] = send(block, block, y_dev(-1))

    def share(c):
        for k in (1, -1, 3, -3, 4):
            got["a", c, k].wait_recv()
        if c == "h":
            got["s", c] = send(hh.at[0], hh.at[1], dev(other=True))
        else:
            got["s", c] = send(hb.at[0, c], hb.at[1, c], dev(other=True))

    def back_product(c):
        got["s", c].wait_recv()
        total = None
        for h in range(2):
            for q, name in enumerate(("wg", "wu")):
                term = dot_nt(hb[h, c, :, q].reshape(NZ * t, f), buf[name][h])
                total = term if total is None else total + term
        total = total.reshape(NZ, t, w)
        zs, zr = buf["zs"], buf["zr"]
        buf["dx"][c] = total[0]
        for k in range(1, NZ):
            zs[c, k] = total[k].astype(BF)
        for k in (4, 3, 5, 2, 6, 1, 7):
            got["zr", c, k] = send(zs.at[c, k], zr.at[c, k], dev(dz=-k))

    def over_z(c):
        total = buf["dx"][c]
        for k in range(1, NZ):
            got["zr", c, k].wait_recv()
            total = total + buf["zr"][c, k].astype(F32)
        return total

    def over_x(c):
        buf["dx"][c] = over_z(c)
        got["xr", c] = send(buf["dx"].at[c], buf["xr"].at[c], dev(dx=-c))

    def weight_grads():
        left = xb[...].reshape(NX * NZ * t, w)
        for h in range(2):
            for q, name, out in ((0, "og", og_hbm), (1, "ou", ou_hbm)):
                right = hb[h, :, :, q].reshape(NX * NZ * t, f)
                buf[name][h] = dot_tn(left, right).astype(BF)
                stores.append(local(buf[name].at[h], out.at[:, halves[h]]))

    def down_grad():
        right = gb[...].reshape(NX * NZ * t, w)
        got["s", "h"].wait_recv()
        for h in range(2):
            left = jnp.concatenate([hh[h, :, c].reshape(NY * t, f) for c in range(NX)], axis=0)
            buf["od"][h] = dot_tn(left, right).astype(BF)
            stores.append(local(buf["od"].at[h], od_hbm.at[halves[h], :]))

    def finish():
        total = over_z(0)
        for c in range(1, NX):
            got["xr", c].wait_recv()
            total = total + buf["xr"][c]
        dx_ref[...] = total.astype(BF)

    first("x", 2)
    first("g", 2)
    column("x")
    first("x", 1)
    first("x", 3)
    column("g")
    first("g", 1)
    first("g", 3)
    for copy in loads:
        copy.wait()
    forward("x", True)
    forward("x", False)
    across("x")
    products(0, 0)
    leaf(0, 0)
    forward("g", True)
    forward("g", False)
    across("g")
    products(0, 1)
    leaf(0, 1)
    arrive(1, "x")
    products(1, 0)
    arrive(3, "x")
    products(3, 0)
    leaf(1, 0)
    leaf(3, 0)
    relay(0, 0)
    arrive(2, "x")
    products(2, 0)
    relay(0, 1)
    leaf(2, 0)
    arrive(1, "g")
    products(1, 1)
    arrive(3, "g")
    products(3, 1)
    relay(1, 0)
    leaf(1, 1)
    relay(3, 0)
    leaf(3, 1)
    owner(0)
    spread(0)
    arrive(2, "g")
    products(2, 1)
    relay(2, 0)
    leaf(2, 1)
    relay(1, 1)
    relay(3, 1)
    owner(1)
    spread(1)
    owner(3)
    spread(3)
    pass_on(0)
    relay(2, 1)
    share(0)
    owner(2)
    spread(2)
    back_product(0)
    pass_on(1)
    pass_on(3)
    spread("h")
    share(1)
    back_product(1)
    share(3)
    back_product(3)
    pass_on(2)
    share(2)
    back_product(2)
    pass_on("h")
    weight_grads()
    over_x(1)
    over_x(3)
    over_x(2)
    share("h")
    down_grad()
    finish()
    for copy in started:
        copy.wait_send()
    for copy in stores:
        copy.wait()


def copies(*refs):
    sem = refs[-1]
    n = len(refs) // 2
    started = []
    for i in range(n):
        src, dst = refs[i], refs[n + i]
        parts = 8 if src.shape[0] % 128 == 0 else 1
        rows = src.shape[0] // parts
        for p in range(parts):
            part = pl.ds(p * rows, rows)
            started.append(pltpu.make_async_copy(src.at[part], dst.at[part], sem.at[len(started)]))
            started[-1].start()
    for copy in started:
        copy.wait()


def per_device(inputs, out_grad, gate_weight, up_weight, down_weight):
    t, w = inputs.shape
    f = gate_weight.shape[1] // 2
    buffers = scratch(t, w, f)
    vmem, hbm = pl.BlockSpec(memory_space=pltpu.VMEM), pl.BlockSpec(memory_space=pl.ANY)
    flops = 2 * 8 * (NX * NZ * t) * w * (2 * f)
    made = pl.pallas_call(
        functools.partial(kernel, list(buffers)),
        out_shape=(
            jax.ShapeDtypeStruct(inputs.shape, BF),
            jax.ShapeDtypeStruct(gate_weight.shape, BF),
            jax.ShapeDtypeStruct(up_weight.shape, BF),
            jax.ShapeDtypeStruct(down_weight.shape, BF),
        ),
        in_specs=[vmem, vmem, hbm, hbm, hbm],
        out_specs=(vmem, hbm, hbm, hbm),
        scratch_shapes=[pltpu.VMEM(shape, dtype) for shape, dtype in buffers.values()]
        + [
            pltpu.SemaphoreType.DMA((N_REMOTE,)),
            pltpu.SemaphoreType.DMA((N_REMOTE,)),
            pltpu.SemaphoreType.DMA((N_LOCAL,)),
        ],
        compiler_params=pltpu.CompilerParams(collective_id=0, has_side_effects=True, vmem_limit_bytes=56 << 20),
        cost_estimate=pl.CostEstimate(flops=flops, bytes_accessed=4 << 20, transcendentals=3 * NX * t * f),
    )(inputs, out_grad, gate_weight, up_weight, down_weight)
    return pl.pallas_call(
        copies,
        out_shape=tuple(jax.ShapeDtypeStruct(a.shape, a.dtype) for a in made),
        in_specs=[hbm] * 4,
        out_specs=(hbm,) * 4,
        scratch_shapes=[pltpu.SemaphoreType.DMA((32,))],
        cost_estimate=pl.CostEstimate(flops=0, bytes_accessed=4 << 20, transcendentals=0),
    )(*made)


def solution(mesh):
    in_specs = (
        P("row", ("inw", "outw")),
        P("row", ("inw", "outw")),
        P(("inw", "outw"), "row"),
        P(("inw", "outw"), "row"),
        P("row", ("inw", "outw")),
    )
    out_specs = (
        P("row", ("inw", "outw")),
        P(("inw", "outw"), "row"),
        P(("inw", "outw"), "row"),
        P("row", ("inw", "outw")),
    )
    return jax.shard_map(per_device, mesh=mesh, in_specs=in_specs, out_specs=out_specs, check_vma=False)
```

```python
import functools

import jax
import jax.numpy as jnp
from jax import lax
from jax.experimental import pallas as pl
from jax.experimental.pallas import tpu as pltpu
from jax.sharding import PartitionSpec as P

MESH = pl.DeviceIdType.MESH
BF, F32 = jnp.bfloat16, jnp.float32
NZ, NX, NY = 8, 4, 8
GROUPS = {c: ((0, 1), (2,)) for c in range(NX)}


def dot(a, b):
    return jnp.dot(a, b, preferred_element_type=F32)


def dot_nt(a, b):
    return lax.dot_general(a, b, (((1,), (1,)), ((), ())), preferred_element_type=F32)


def dot_tn(a, b):
    return lax.dot_general(a, b, (((0,), (0,)), ((), ())), preferred_element_type=F32)


def scratch(t, w, f):
    made = {
        "xb": ((NX, NZ, t, w), BF),
        "gb": ((NX, NZ, t, w), BF),
        "wg": ((2, w, f), BF),
        "wu": ((2, w, f), BF),
        "wd": ((2, f, w), BF),
        "hb": ((2, NX, NZ, 2, t, f), BF),
        "hh": ((2, NY, NX, t, f), BF),
        "dx": ((NX, t, w), F32),
        "xr": ((NX, t, w), F32),
        "d0": ((NZ, t, w), F32),
        "xs": ((NX, NZ, t, w), BF),
        "xq": ((NX, NZ, t, w), BF),
        "zs": ((NX, NZ, t, w), BF),
        "zr": ((NX, NZ, t, w), BF),
        "og": ((2, w, f), BF),
        "ou": ((2, w, f), BF),
        "od": ((2, f, w), BF),
    }
    for c, groups in GROUPS.items():
        for g, qs in enumerate(groups):
            n = len(qs)
            made[f"po{c}{g}"] = ((NZ, n, t, f), F32)
            made[f"cs{c}{g}"] = ((NZ, n, t, f), F32)
            made[f"cr{c}{g}"] = ((NZ, n, t, f), F32)
            made[f"pb{c}{g}"] = ((NZ, n, t, f), BF)
            made[f"rr{c}{g}"] = ((3, n, t, f), BF)
            made[f"sr{c}{g}"] = ((2, n, t, f), BF)
            made[f"ro{c}{g}"] = ((4, n, t, f), BF)
    return made


N_REMOTE = 256
N_LOCAL = 16


def kernel(names, x_ref, g_ref, wg_hbm, wu_hbm, wd_hbm, dx_ref, og_hbm, ou_hbm, od_hbm, *refs):
    buf = dict(zip(names, refs))
    ssem, rsem, lsem = refs[len(names) :]
    t, w = x_ref.shape
    f = wg_hbm.shape[1] // 2
    row, inw, outw = lax.axis_index("row"), lax.axis_index("inw"), lax.axis_index("outw")
    z, x = row // NX, row % NX
    y, core = outw * 4 + inw // 2, inw % 2
    s = 1 - 2 * core

    def dev(dz=0, dx=0, dy=0, other=False):
        zz, xx, yy = (z + dz + NZ) % NZ, (x + dx + NX) % NX, (y + dy + NY) % NY
        cc = 1 - core if other else core
        return (zz * NX + xx, (yy % 4) * 2 + cc, yy // 4)

    def at_y(k):
        return (y + k * s + NY) % NY

    def y_dev(k):
        return dev(dy=k * s)

    started, used = [], [0, 0]

    def send(src, dst, device):
        i = used[0]
        used[0] += 1
        copy = pltpu.make_async_remote_copy(
            src_ref=src, dst_ref=dst, send_sem=ssem.at[i], recv_sem=rsem.at[i], device_id=device, device_id_type=MESH
        )
        copy.start()
        started.append(copy)
        return copy

    def local(src, dst):
        i = used[1]
        used[1] += 1
        copy = pltpu.make_async_copy(src, dst, lsem.at[i])
        copy.start()
        return copy

    halves = [pl.ds(pl.multiple_of(h * f, f), f) for h in (core, 1 - core)]
    loads = []
    for h in range(2):
        loads.append(local(wg_hbm.at[:, halves[h]], buf["wg"].at[h]))
        loads.append(local(wu_hbm.at[:, halves[h]], buf["wu"].at[h]))
        loads.append(local(wd_hbm.at[halves[h], :], buf["wd"].at[h]))

    barrier = pltpu.get_barrier_semaphore()
    peers = [dev(dz=k) for k in range(1, NZ)] + [dev(dx=k) for k in range(1, NX)]
    peers += [dev(dy=k) for k in (1, -1, 2, -2)] + [dev(other=True)]
    for peer in peers:
        pl.semaphore_signal(barrier, inc=1, device_id=peer, device_id_type=MESH)
    xb, gb, hb, hh = buf["xb"], buf["gb"], buf["hb"], buf["hh"]
    xb[0, 0] = x_ref[...]
    gb[0, 0] = g_ref[...]
    pl.semaphore_wait(barrier, len(peers))

    got = {}
    stores = []
    blocks = {"x": (x_ref, xb), "g": (g_ref, gb)}

    def first(name, c):
        ref, block = blocks[name]
        got[name, c, 0] = send(ref, block.at[c, 0], dev(dx=c))

    def column(name):
        ref, block = blocks[name]
        for k in (1, 7, 2, 6, 3, 5, 4):
            got[name, 0, k] = send(ref, block.at[0, k], dev(dz=k))

    def forward(name, near):
        block = blocks[name][1]
        for k in (1, 7, 2, 6) if near else (3, 5, 4):
            got[name, 0, k].wait_recv()
        for start, size in ((1, 2), (6, 2)) if near else ((3, 3),):
            for c in (1, 3):
                part = pl.ds(start, size)
                got[name, c, start] = send(block.at[0, part], block.at[c, part], dev(dx=c))

    def across(name):
        block = blocks[name][1]
        got[name, 2, 0].wait_recv()
        for k in (1, 7, 2, 6, 3, 5, 4):
            got[name, 2, k] = send(block.at[2, 0], block.at[2, k], dev(dz=k))

    def arrive(c, name):
        for k in range(1, NZ) if c == 2 else (0, 1, 6, 3):
            got[name, c, k].wait_recv()

    def products(c, g):
        if c:
            for name in sorted({"g" if q == 2 else "x" for q in GROUPS[c][g]}):
                arrive(c, name)
        for i, q in enumerate(GROUPS[c][g]):
            left = (gb if q == 2 else xb)[c].reshape(NZ * t, w)
            for h in (1, 0):
                if q == 2:
                    part = dot_nt(left, buf["wd"][h])
                else:
                    part = dot(left, buf["wu" if q else "wg"][h])
                to = buf[f"{'cs' if h else 'po'}{c}{g}"]
                to[:, i] = part.reshape(NZ, t, f)
        got["c", c, g] = send(buf[f"cs{c}{g}"], buf[f"cr{c}{g}"], dev(other=True))

    def own(c, g, slot):
        return buf[f"po{c}{g}"][slot] + buf[f"cr{c}{g}"][slot]

    def leaf(c, g):
        got["c", c, g].wait_recv()
        pb, rr, ro = buf[f"pb{c}{g}"], buf[f"rr{c}{g}"], buf[f"ro{c}{g}"]
        for slot in range(NZ):
            pb[slot] = own(c, g, slot).astype(BF)
        got["l", c, g] = [
            send(pb.at[at_y(-3)], rr.at[0], y_dev(-1)),
            send(pb.at[at_y(-4)], rr.at[1], y_dev(-2)),
            send(pb.at[at_y(3)], rr.at[2], y_dev(1)),
        ]
        got["d", c, g] = [send(pb.at[at_y(-1)], ro.at[0], y_dev(-1)), send(pb.at[at_y(1)], ro.at[1], y_dev(1))]

    def relay(c, g):
        for copy in got["l", c, g]:
            copy.wait_recv()
        rr, sr, ro = buf[f"rr{c}{g}"], buf[f"sr{c}{g}"], buf[f"ro{c}{g}"]
        sr[0] = (own(c, g, at_y(-2)) + rr[0].astype(F32) + rr[1].astype(F32)).astype(BF)
        one = send(sr.at[0], ro.at[2], y_dev(-2))
        sr[1] = (own(c, g, at_y(2)) + rr[2].astype(F32)).astype(BF)
        got["d", c, g] += [one, send(sr.at[1], ro.at[3], y_dev(2))]

    def owner(c):
        sums = {}
        for g, qs in enumerate(GROUPS[c]):
            for copy in got["d", c, g]:
                copy.wait_recv()
            total = own(c, g, y)
            for i in range(4):
                total = total + buf[f"ro{c}{g}"][i].astype(F32)
            for i, q in enumerate(qs):
                sums[q] = total[i]
        gate, up, back = sums[0], sums[1], sums[2]
        sig = jax.nn.sigmoid(gate)
        silu = gate * sig
        hb[0, c, y, 0] = (back * up * sig * (1.0 + gate * (1.0 - sig))).astype(BF)
        hb[0, c, y, 1] = (back * silu).astype(BF)
        hh[0, y, c] = (silu * up).astype(BF)

    def result(c, slot):
        return hh.at[0, slot] if c == "h" else hb.at[0, c, slot]

    def spread(c):
        mine = result(c, y)
        for k in (2, -2, 1, -1):
            got["a", c, k] = send(mine, mine, y_dev(k))

    def pass_on(c):
        got["a", c, 2].wait_recv()
        block = result(c, at_y(-2))
        got["a", c, 4] = send(block, block, y_dev(2))
        got["a", c, 3] = send(block, block, y_dev(1))
        got["a", c, -2].wait_recv()
        block = result(c, at_y(2))
        got["a", c, -3] = send(block, block, y_dev(-1))

    def share(c):
        for k in (1, -1, 3, -3, 4):
            got["a", c, k].wait_recv()
        if c == "h":
            got["s", c] = send(hh.at[0], hh.at[1], dev(other=True))
        else:
            got["s", c] = send(hb.at[0, c], hb.at[1, c], dev(other=True))

    def back_product(c):
        got["s", c].wait_recv()
        total = None
        for h in range(2):
            for q, name in enumerate(("wg", "wu")):
                term = dot_nt(hb[h, c, :, q].reshape(NZ * t, f), buf[name][h])
                total = term if total is None else total + term
        total = total.reshape(NZ, t, w)
        if c in (1, 3):
            buf["xs"][c] = total.astype(BF)
            got["xq", c] = send(buf["xs"].at[c], buf["xq"].at[c], dev(dx=-c))
        elif c == 0:
            buf["d0"][...] = total
        else:
            to_z(c, lambda k: total[k])

    def to_z(c, block):
        zs, zr = buf["zs"], buf["zr"]
        for k in (4, 3, 5, 2, 6, 1, 7):
            zs[c, k] = block(k).astype(BF)
            got["zr", c, k] = send(zs.at[c, k], zr.at[c, k], dev(dz=-k))
        buf["dx"][c] = block(0)

    def mix():
        for c in (1, 3):
            got["xq", c].wait_recv()
        xq = buf["xq"]
        to_z(0, lambda k: buf["d0"][k] + xq[1, k].astype(F32) + xq[3, k].astype(F32))

    def over_z(c):
        total = buf["dx"][c]
        for k in range(1, NZ):
            got["zr", c, k].wait_recv()
            total = total + buf["zr"][c, k].astype(F32)
        return total

    def over_x(c):
        buf["dx"][c] = over_z(c)
        got["xr", c] = send(buf["dx"].at[c], buf["xr"].at[c], dev(dx=-c))

    def weight_grads():
        left = xb[...].reshape(NX * NZ * t, w)
        for h in range(2):
            for q, name, out in ((0, "og", og_hbm), (1, "ou", ou_hbm)):
                right = hb[h, :, :, q].reshape(NX * NZ * t, f)
                buf[name][h] = dot_tn(left, right).astype(BF)
                stores.append(local(buf[name].at[h], out.at[:, halves[h]]))

    def down_grad():
        right = gb[...].reshape(NX * NZ * t, w)
        got["s", "h"].wait_recv()
        for h in range(2):
            left = jnp.concatenate([hh[h, :, c].reshape(NY * t, f) for c in range(NX)], axis=0)
            buf["od"][h] = dot_tn(left, right).astype(BF)
            stores.append(local(buf["od"].at[h], od_hbm.at[halves[h], :]))

    def finish():
        total = over_z(0)
        got["xr", 2].wait_recv()
        total = total + buf["xr"][2]
        dx_ref[...] = total.astype(BF)

    first("x", 2)
    first("g", 2)
    column("x")
    first("x", 1)
    first("x", 3)
    column("g")
    first("g", 1)
    first("g", 3)
    for copy in loads:
        copy.wait()
    across("x")
    forward("x", True)
    forward("x", False)
    across("g")
    products(0, 0)
    leaf(0, 0)
    forward("g", True)
    forward("g", False)
    products(0, 1)
    products(1, 0)
    products(3, 0)
    leaf(0, 1)
    leaf(1, 0)
    relay(0, 0)
    products(2, 0)
    leaf(3, 0)
    products(1, 1)
    products(3, 1)
    relay(0, 1)
    leaf(1, 1)
    leaf(3, 1)
    products(2, 1)
    leaf(2, 0)
    leaf(2, 1)
    relay(1, 0)
    relay(1, 1)
    relay(3, 0)
    owner(0)
    relay(3, 1)
    relay(2, 0)
    relay(2, 1)
    spread(0)
    owner(1)
    spread(1)
    owner(3)
    spread(3)
    owner(2)
    spread(2)
    pass_on(1)
    pass_on(3)
    pass_on(2)
    pass_on(0)
    share(1)
    back_product(1)
    share(3)
    spread("h")
    share(2)
    back_product(3)
    share(0)
    back_product(2)
    back_product(0)
    weight_grads()
    pass_on("h")
    mix()
    over_x(2)
    share("h")
    down_grad()
    finish()
    for copy in started:
        copy.wait_send()
    for copy in stores:
        copy.wait()


def copies(*refs):
    n = len(refs) // 3
    came, went = refs[3 * n :]
    parts = []
    for src, dst, held in zip(refs[:n], refs[n : 2 * n], refs[2 * n : 3 * n]):
        pieces = 4 if src.shape[0] % 64 == 0 else 1
        rows = src.shape[0] // pieces
        for p in range(pieces):
            part, i = pl.ds(p * rows, rows), len(parts)
            inward = pltpu.make_async_copy(src.at[part], held.at[part], came.at[i])
            parts.append((inward, pltpu.make_async_copy(held.at[part], dst.at[part], went.at[i])))
            inward.start()
    for inward, outward in parts:
        inward.wait()
        outward.start()
    for inward, outward in parts:
        outward.wait()


def per_device(inputs, out_grad, gate_weight, up_weight, down_weight):
    t, w = inputs.shape
    f = gate_weight.shape[1] // 2
    buffers = scratch(t, w, f)
    vmem, hbm = pl.BlockSpec(memory_space=pltpu.VMEM), pl.BlockSpec(memory_space=pl.ANY)
    flops = 2 * 8 * (NX * NZ * t) * w * (2 * f)
    made = pl.pallas_call(
        functools.partial(kernel, list(buffers)),
        out_shape=(
            jax.ShapeDtypeStruct(inputs.shape, BF),
            jax.ShapeDtypeStruct(gate_weight.shape, BF),
            jax.ShapeDtypeStruct(up_weight.shape, BF),
            jax.ShapeDtypeStruct(down_weight.shape, BF),
        ),
        in_specs=[vmem, vmem, hbm, hbm, hbm],
        out_specs=(vmem, hbm, hbm, hbm),
        scratch_shapes=[pltpu.VMEM(shape, dtype) for shape, dtype in buffers.values()]
        + [
            pltpu.SemaphoreType.DMA((N_REMOTE,)),
            pltpu.SemaphoreType.DMA((N_REMOTE,)),
            pltpu.SemaphoreType.DMA((N_LOCAL,)),
        ],
        compiler_params=pltpu.CompilerParams(collective_id=0, has_side_effects=True, vmem_limit_bytes=56 << 20),
        cost_estimate=pl.CostEstimate(flops=flops, bytes_accessed=4 << 20, transcendentals=3 * NX * t * f),
    )(inputs, out_grad, gate_weight, up_weight, down_weight)
    return pl.pallas_call(
        copies,
        out_shape=tuple(jax.ShapeDtypeStruct(a.shape, a.dtype) for a in made),
        in_specs=[hbm] * 4,
        out_specs=(hbm,) * 4,
        scratch_shapes=[pltpu.VMEM(a.shape, a.dtype) for a in made]
        + [pltpu.SemaphoreType.DMA((16,)), pltpu.SemaphoreType.DMA((16,))],
        cost_estimate=pl.CostEstimate(flops=0, bytes_accessed=4 << 20, transcendentals=0),
    )(*made)


def solution(mesh):
    in_specs = (
        P("row", ("inw", "outw")),
        P("row", ("inw", "outw")),
        P(("inw", "outw"), "row"),
        P(("inw", "outw"), "row"),
        P("row", ("inw", "outw")),
    )
    out_specs = (
        P("row", ("inw", "outw")),
        P(("inw", "outw"), "row"),
        P(("inw", "outw"), "row"),
        P("row", ("inw", "outw")),
    )
    return jax.shard_map(per_device, mesh=mesh, in_specs=in_specs, out_specs=out_specs, check_vma=False)
```

```python
import functools

import jax
import jax.numpy as jnp
from jax import lax
from jax.experimental import pallas as pl
from jax.experimental.pallas import tpu as pltpu
from jax.sharding import PartitionSpec as P

MESH = pl.DeviceIdType.MESH
BF, F32 = jnp.bfloat16, jnp.float32
NZ, NX, NY = 8, 4, 8
GROUPS = {c: ((0, 1), (2,)) for c in range(NX)}


def dot(a, b):
    return jnp.dot(a, b, preferred_element_type=F32)


def dot_nt(a, b):
    return lax.dot_general(a, b, (((1,), (1,)), ((), ())), preferred_element_type=F32)


def dot_tn(a, b):
    return lax.dot_general(a, b, (((0,), (0,)), ((), ())), preferred_element_type=F32)


def scratch(t, w, f):
    made = {
        "xb": ((NX, NZ, t, w), BF),
        "gb": ((NX, NZ, t, w), BF),
        "wg": ((2, w, f), BF),
        "wu": ((2, w, f), BF),
        "wd": ((2, f, w), BF),
        "hb": ((2, NX, NZ, 2, t, f), BF),
        "hh": ((2, NY, NX, t, f), BF),
        "dx": ((NX, t, w), F32),
        "xr": ((NX, t, w), F32),
        "d0": ((NZ, t, w), F32),
        "xs": ((NX, NZ, t, w), BF),
        "xq": ((NX, NZ, t, w), BF),
        "zs": ((NX, NZ, t, w), BF),
        "zr": ((NX, NZ, t, w), BF),
    }
    for c, groups in GROUPS.items():
        for g, qs in enumerate(groups):
            n = len(qs)
            made[f"po{c}{g}"] = ((NZ, n, t, f), F32)
            made[f"cs{c}{g}"] = ((NZ, n, t, f), F32)
            made[f"cr{c}{g}"] = ((NZ, n, t, f), F32)
            made[f"pb{c}{g}"] = ((NZ, n, t, f), BF)
            made[f"rr{c}{g}"] = ((3, n, t, f), BF)
            made[f"sr{c}{g}"] = ((2, n, t, f), BF)
            made[f"ro{c}{g}"] = ((4, n, t, f), BF)
    return made


N_REMOTE = 256
N_LOCAL = 16


def kernel(names, x_ref, g_ref, wg_hbm, wu_hbm, wd_hbm, dx_ref, og_ref, ou_ref, od_ref, *refs):
    buf = dict(zip(names, refs))
    ssem, rsem, lsem = refs[len(names) :]
    t, w = x_ref.shape
    f = wg_hbm.shape[1] // 2
    row, inw, outw = lax.axis_index("row"), lax.axis_index("inw"), lax.axis_index("outw")
    z, x = row // NX, row % NX
    y, core = outw * 4 + inw // 2, inw % 2
    s = 1 - 2 * core

    def dev(dz=0, dx=0, dy=0, other=False):
        zz, xx, yy = (z + dz + NZ) % NZ, (x + dx + NX) % NX, (y + dy + NY) % NY
        cc = 1 - core if other else core
        return (zz * NX + xx, (yy % 4) * 2 + cc, yy // 4)

    def at_y(k):
        return (y + k * s + NY) % NY

    def y_dev(k):
        return dev(dy=k * s)

    started, used = [], [0, 0]

    def send(src, dst, device):
        i = used[0]
        used[0] += 1
        copy = pltpu.make_async_remote_copy(
            src_ref=src, dst_ref=dst, send_sem=ssem.at[i], recv_sem=rsem.at[i], device_id=device, device_id_type=MESH
        )
        copy.start()
        started.append(copy)
        return copy

    def local(src, dst):
        i = used[1]
        used[1] += 1
        copy = pltpu.make_async_copy(src, dst, lsem.at[i])
        copy.start()
        return copy

    halves = [pl.ds(pl.multiple_of(h * f, f), f) for h in (core, 1 - core)]
    loads = []
    for h in range(2):
        loads.append(local(wg_hbm.at[:, halves[h]], buf["wg"].at[h]))
        loads.append(local(wu_hbm.at[:, halves[h]], buf["wu"].at[h]))
        loads.append(local(wd_hbm.at[halves[h], :], buf["wd"].at[h]))

    barrier = pltpu.get_barrier_semaphore()
    peers = [dev(dz=k) for k in range(1, NZ)] + [dev(dx=k) for k in range(1, NX)]
    peers += [dev(dy=k) for k in (1, -1, 2, -2)] + [dev(other=True)]
    for peer in peers:
        pl.semaphore_signal(barrier, inc=1, device_id=peer, device_id_type=MESH)
    xb, gb, hb, hh = buf["xb"], buf["gb"], buf["hb"], buf["hh"]
    xb[0, 0] = x_ref[...]
    gb[0, 0] = g_ref[...]
    pl.semaphore_wait(barrier, len(peers))

    got = {}
    blocks = {"x": (x_ref, xb), "g": (g_ref, gb)}

    def first(name, c):
        ref, block = blocks[name]
        got[name, c, 0] = send(ref, block.at[c, 0], dev(dx=c))

    def column(name):
        ref, block = blocks[name]
        for k in (4, 3, 5, 2, 6, 1, 7):
            got[name, 0, k] = send(ref, block.at[0, k], dev(dz=k))

    def forward(name, near):
        block = blocks[name][1]
        for k in (1, 7, 2, 6) if near else (3, 5, 4):
            got[name, 0, k].wait_recv()
        for start, size in ((1, 2), (6, 2)) if near else ((3, 3),):
            for c in (1, 3):
                part = pl.ds(start, size)
                got[name, c, start] = send(block.at[0, part], block.at[c, part], dev(dx=c))

    def across(name):
        block = blocks[name][1]
        got[name, 2, 0].wait_recv()
        for k in (4, 3, 5, 2, 6, 1, 7):
            got[name, 2, k] = send(block.at[2, 0], block.at[2, k], dev(dz=k))

    def arrive(c, name):
        for k in range(1, NZ) if c == 2 else (0, 1, 6, 3):
            got[name, c, k].wait_recv()

    def products(c, g):
        if c:
            for name in sorted({"g" if q == 2 else "x" for q in GROUPS[c][g]}):
                arrive(c, name)
        for i, q in enumerate(GROUPS[c][g]):
            left = (gb if q == 2 else xb)[c].reshape(NZ * t, w)
            for h in (1, 0):
                if q == 2:
                    part = dot_nt(left, buf["wd"][h])
                else:
                    part = dot(left, buf["wu" if q else "wg"][h])
                to = buf[f"{'cs' if h else 'po'}{c}{g}"]
                to[:, i] = part.reshape(NZ, t, f)
        got["c", c, g] = send(buf[f"cs{c}{g}"], buf[f"cr{c}{g}"], dev(other=True))

    def own(c, g, slot):
        return buf[f"po{c}{g}"][slot] + buf[f"cr{c}{g}"][slot]

    def leaf(c, g):
        got["c", c, g].wait_recv()
        pb, rr, ro = buf[f"pb{c}{g}"], buf[f"rr{c}{g}"], buf[f"ro{c}{g}"]
        for slot in range(NZ):
            pb[slot] = own(c, g, slot).astype(BF)
        got["l", c, g] = [
            send(pb.at[at_y(-3)], rr.at[0], y_dev(-1)),
            send(pb.at[at_y(-4)], rr.at[1], y_dev(-2)),
            send(pb.at[at_y(3)], rr.at[2], y_dev(1)),
        ]
        got["d", c, g] = [send(pb.at[at_y(-1)], ro.at[0], y_dev(-1)), send(pb.at[at_y(1)], ro.at[1], y_dev(1))]

    def relay(c, g):
        for copy in got["l", c, g]:
            copy.wait_recv()
        rr, sr, ro = buf[f"rr{c}{g}"], buf[f"sr{c}{g}"], buf[f"ro{c}{g}"]
        sr[0] = (own(c, g, at_y(-2)) + rr[0].astype(F32) + rr[1].astype(F32)).astype(BF)
        one = send(sr.at[0], ro.at[2], y_dev(-2))
        sr[1] = (own(c, g, at_y(2)) + rr[2].astype(F32)).astype(BF)
        got["d", c, g] += [one, send(sr.at[1], ro.at[3], y_dev(2))]

    def owner(c):
        sums = {}
        for g, qs in enumerate(GROUPS[c]):
            for copy in got["d", c, g]:
                copy.wait_recv()
            total = own(c, g, y)
            for i in range(4):
                total = total + buf[f"ro{c}{g}"][i].astype(F32)
            for i, q in enumerate(qs):
                sums[q] = total[i]
        gate, up, back = sums[0], sums[1], sums[2]
        sig = jax.nn.sigmoid(gate)
        silu = gate * sig
        hb[0, c, y, 0] = (back * up * sig * (1.0 + gate * (1.0 - sig))).astype(BF)
        hb[0, c, y, 1] = (back * silu).astype(BF)
        hh[0, y, c] = (silu * up).astype(BF)

    def result(c, slot):
        return hh.at[0, slot] if c == "h" else hb.at[0, c, slot]

    def spread(c):
        mine = result(c, y)
        for k in (2, -2, 1, -1):
            got["a", c, k] = send(mine, mine, y_dev(k))

    def pass_on(c):
        got["a", c, 2].wait_recv()
        block = result(c, at_y(-2))
        got["a", c, 4] = send(block, block, y_dev(2))
        got["a", c, 3] = send(block, block, y_dev(1))
        got["a", c, -2].wait_recv()
        block = result(c, at_y(2))
        got["a", c, -3] = send(block, block, y_dev(-1))

    def share(c):
        for k in (1, -1, 3, -3, 4):
            got["a", c, k].wait_recv()
        if c == "h":
            got["s", c] = send(hh.at[0], hh.at[1], dev(other=True))
        else:
            got["s", c] = send(hb.at[0, c], hb.at[1, c], dev(other=True))

    def back_product(c):
        got["s", c].wait_recv()
        total = None
        for h in range(2):
            for q, name in enumerate(("wg", "wu")):
                term = dot_nt(hb[h, c, :, q].reshape(NZ * t, f), buf[name][h])
                total = term if total is None else total + term
        total = total.reshape(NZ, t, w)
        if c in (1, 3):
            buf["xs"][c] = total.astype(BF)
            got["xq", c] = send(buf["xs"].at[c], buf["xq"].at[c], dev(dx=-c))
        elif c == 0:
            buf["d0"][...] = total
        else:
            to_z(c, lambda k: total[k])

    def to_z(c, block):
        zs, zr = buf["zs"], buf["zr"]
        for k in (4, 3, 5, 2, 6, 1, 7):
            zs[c, k] = block(k).astype(BF)
            got["zr", c, k] = send(zs.at[c, k], zr.at[c, k], dev(dz=-k))
        buf["dx"][c] = block(0)

    def mix():
        for c in (1, 3):
            got["xq", c].wait_recv()
        xq = buf["xq"]
        to_z(0, lambda k: buf["d0"][k] + xq[1, k].astype(F32) + xq[3, k].astype(F32))

    def over_z(c):
        total = buf["dx"][c]
        for k in range(1, NZ):
            got["zr", c, k].wait_recv()
            total = total + buf["zr"][c, k].astype(F32)
        return total

    def over_x(c):
        buf["dx"][c] = over_z(c)
        got["xr", c] = send(buf["dx"].at[c], buf["xr"].at[c], dev(dx=-c))

    def weight_grads():
        left = xb[...].reshape(NX * NZ * t, w)
        for h in range(2):
            for q, out in ((0, og_ref), (1, ou_ref)):
                right = hb[h, :, :, q].reshape(NX * NZ * t, f)
                out[:, halves[h]] = dot_tn(left, right).astype(BF)

    def down_grad():
        right = gb[...].reshape(NX * NZ * t, w)
        got["s", "h"].wait_recv()
        for h in range(2):
            left = jnp.concatenate([hh[h, :, c].reshape(NY * t, f) for c in range(NX)], axis=0)
            od_ref[halves[h], :] = dot_tn(left, right).astype(BF)

    def finish():
        total = over_z(0)
        got["xr", 2].wait_recv()
        total = total + buf["xr"][2]
        dx_ref[...] = total.astype(BF)

    first("x", 2)
    first("g", 2)
    column("x")
    first("x", 1)
    first("x", 3)
    column("g")
    first("g", 1)
    first("g", 3)
    for copy in loads:
        copy.wait()
    across("x")
    across("g")
    forward("x", False)
    forward("x", True)
    products(0, 0)
    leaf(0, 0)
    forward("g", False)
    forward("g", True)
    products(0, 1)
    products(1, 0)
    leaf(0, 1)
    relay(0, 0)
    products(3, 0)
    leaf(1, 0)
    leaf(3, 0)
    products(1, 1)
    products(3, 1)
    products(2, 0)
    relay(0, 1)
    leaf(1, 1)
    products(2, 1)
    leaf(3, 1)
    leaf(2, 0)
    leaf(2, 1)
    relay(1, 0)
    relay(1, 1)
    owner(0)
    relay(3, 1)
    relay(3, 0)
    relay(2, 0)
    relay(2, 1)
    spread(0)
    owner(1)
    spread(1)
    owner(3)
    spread(3)
    owner(2)
    spread(2)
    pass_on(1)
    pass_on(0)
    pass_on(3)
    pass_on(2)
    spread("h")
    share(1)
    back_product(1)
    share(3)
    share(2)
    share(0)
    back_product(3)
    back_product(2)
    back_product(0)
    weight_grads()
    pass_on("h")
    mix()
    share("h")
    over_x(2)
    down_grad()
    finish()
    for copy in started:
        copy.wait_send()


def copies(*refs):
    n, sem = len(refs) // 2, refs[-1]
    started = [pltpu.make_async_copy(refs[i], refs[n + i], sem.at[i]) for i in range(n)]
    for copy in started:
        copy.start()
    for copy in started:
        copy.wait()


def per_device(inputs, out_grad, gate_weight, up_weight, down_weight):
    t, w = inputs.shape
    f = gate_weight.shape[1] // 2
    buffers = scratch(t, w, f)
    vmem, hbm = pl.BlockSpec(memory_space=pltpu.VMEM), pl.BlockSpec(memory_space=pl.ANY)
    flops = 2 * 8 * (NX * NZ * t) * w * (2 * f)
    made = pl.pallas_call(
        functools.partial(kernel, list(buffers)),
        out_shape=(
            pltpu.VMEM(inputs.shape, BF),
            pltpu.VMEM(gate_weight.shape, BF),
            pltpu.VMEM(up_weight.shape, BF),
            pltpu.VMEM(down_weight.shape, BF),
        ),
        in_specs=[vmem, vmem, hbm, hbm, hbm],
        out_specs=(vmem,) * 4,
        scratch_shapes=[pltpu.VMEM(shape, dtype) for shape, dtype in buffers.values()]
        + [
            pltpu.SemaphoreType.DMA((N_REMOTE,)),
            pltpu.SemaphoreType.DMA((N_REMOTE,)),
            pltpu.SemaphoreType.DMA((N_LOCAL,)),
        ],
        compiler_params=pltpu.CompilerParams(collective_id=0, has_side_effects=True, vmem_limit_bytes=56 << 20),
        cost_estimate=pl.CostEstimate(flops=flops, bytes_accessed=4 << 20, transcendentals=3 * NX * t * f),
    )(inputs, out_grad, gate_weight, up_weight, down_weight)
    return pl.pallas_call(
        copies,
        out_shape=tuple(jax.ShapeDtypeStruct(a.shape, a.dtype) for a in made),
        in_specs=[vmem] * 4,
        out_specs=(hbm,) * 4,
        scratch_shapes=[pltpu.SemaphoreType.DMA((4,))],
        cost_estimate=pl.CostEstimate(flops=0, bytes_accessed=4 << 20, transcendentals=0),
    )(*(pltpu.with_memory_space_constraint(a, pltpu.VMEM) for a in made))

def solution(mesh):
    in_specs = (
        P("row", ("inw", "outw")),
        P("row", ("inw", "outw")),
        P(("inw", "outw"), "row"),
        P(("inw", "outw"), "row"),
        P("row", ("inw", "outw")),
    )
    out_specs = (
        P("row", ("inw", "outw")),
        P(("inw", "outw"), "row"),
        P(("inw", "outw"), "row"),
        P("row", ("inw", "outw")),
    )
    return jax.shard_map(per_device, mesh=mesh, in_specs=in_specs, out_specs=out_specs, check_vma=False)
```

```python
import functools

import jax
import jax.numpy as jnp
from jax import lax
from jax.experimental import pallas as pl
from jax.experimental.pallas import tpu as pltpu
from jax.sharding import PartitionSpec as P

MESH = pl.DeviceIdType.MESH
BF, F32 = jnp.bfloat16, jnp.float32
NZ, NX, NY = 8, 4, 8
GROUPS = {c: ((0, 1), (2,)) for c in range(NX)}


def dot(a, b):
    return jnp.dot(a, b, preferred_element_type=F32)


def dot_nt(a, b):
    return lax.dot_general(a, b, (((1,), (1,)), ((), ())), preferred_element_type=F32)


def dot_tn(a, b):
    return lax.dot_general(a, b, (((0,), (0,)), ((), ())), preferred_element_type=F32)


def scratch(t, w, f):
    made = {
        "xb": ((NX, NZ, t, w), BF),
        "gb": ((NX, NZ, t, w), BF),
        "wg": ((2, w, f), BF),
        "wu": ((2, w, f), BF),
        "wd": ((2, f, w), BF),
        "hb": ((2, NX, NZ, 2, t, f), BF),
        "hh": ((2, NY, NX, t, f), BF),
        "dx": ((NX, t, w), F32),
        "xr": ((NX, t, w), F32),
        "d0": ((NZ, t, w), F32),
        "xs": ((NX, NZ, t, w), BF),
        "xq": ((NX, NZ, t, w), BF),
        "zs": ((NX, NZ, t, w), BF),
        "zr": ((NX, NZ, t, w), BF),
    }
    for c, groups in GROUPS.items():
        for g, qs in enumerate(groups):
            n = len(qs)
            made[f"po{c}{g}"] = ((NZ, n, t, f), F32)
            made[f"cs{c}{g}"] = ((NZ, n, t, f), F32)
            made[f"cr{c}{g}"] = ((NZ, n, t, f), F32)
            made[f"pb{c}{g}"] = ((NZ, n, t, f), BF)
            made[f"rr{c}{g}"] = ((3, n, t, f), BF)
            made[f"sr{c}{g}"] = ((2, n, t, f), BF)
            made[f"ro{c}{g}"] = ((4, n, t, f), BF)
    return made


N_REMOTE = 256
PARTS = ((3, 3), (6, 2), (0, 3))
N_LOCAL = 16


def kernel(names, x_ref, g_ref, wg_hbm, wu_hbm, wd_hbm, dx_ref, og_ref, ou_ref, od_ref, *refs):
    buf = dict(zip(names, refs))
    ssem, rsem, lsem = refs[len(names) :]
    t, w = x_ref.shape
    f = wg_hbm.shape[1] // 2
    row, inw, outw = lax.axis_index("row"), lax.axis_index("inw"), lax.axis_index("outw")
    z, x = row // NX, row % NX
    y, core = outw * 4 + inw // 2, inw % 2
    s = 1 - 2 * core

    def dev(dz=0, dx=0, dy=0, other=False):
        zz, xx, yy = (z + dz + NZ) % NZ, (x + dx + NX) % NX, (y + dy + NY) % NY
        cc = 1 - core if other else core
        return (zz * NX + xx, (yy % 4) * 2 + cc, yy // 4)

    def at_y(k):
        return (y + k * s + NY) % NY

    def y_dev(k):
        return dev(dy=k * s)

    started, used = [], [0, 0]

    def send(src, dst, device):
        i = used[0]
        used[0] += 1
        copy = pltpu.make_async_remote_copy(
            src_ref=src, dst_ref=dst, send_sem=ssem.at[i], recv_sem=rsem.at[i], device_id=device, device_id_type=MESH
        )
        copy.start()
        started.append(copy)
        return copy

    def local(src, dst):
        i = used[1]
        used[1] += 1
        copy = pltpu.make_async_copy(src, dst, lsem.at[i])
        copy.start()
        return copy

    halves = [pl.ds(pl.multiple_of(h * f, f), f) for h in (core, 1 - core)]
    loads = []
    for h in range(2):
        loads.append(local(wg_hbm.at[:, halves[h]], buf["wg"].at[h]))
        loads.append(local(wu_hbm.at[:, halves[h]], buf["wu"].at[h]))
        loads.append(local(wd_hbm.at[halves[h], :], buf["wd"].at[h]))

    barrier = pltpu.get_barrier_semaphore()
    peers = [dev(dz=k) for k in range(1, NZ)] + [dev(dx=k) for k in range(1, NX)]
    peers += [dev(dy=k) for k in (1, -1, 2, -2)] + [dev(other=True)]
    for peer in peers:
        pl.semaphore_signal(barrier, inc=1, device_id=peer, device_id_type=MESH)
    xb, gb, hb, hh = buf["xb"], buf["gb"], buf["hb"], buf["hh"]
    xb[0, 0] = x_ref[...]
    gb[0, 0] = g_ref[...]
    pl.semaphore_wait(barrier, len(peers))

    got = {}
    blocks = {"x": (x_ref, xb), "g": (g_ref, gb)}

    def first(name, c):
        ref, block = blocks[name]
        got[name, c, 0] = send(ref, block.at[c, 0], dev(dx=c))

    def column(name):
        ref, block = blocks[name]
        for k in (4, 3, 5, 2, 6, 1, 7):
            got[name, 0, k] = send(ref, block.at[0, k], dev(dz=k))

    def forward(name, near):
        block = blocks[name][1]
        for k in (1, 7, 2, 6) if near else (3, 5, 4):
            got[name, 0, k].wait_recv()
        for start, size in ((1, 2), (6, 2)) if near else ((3, 3),):
            for c in (1, 3):
                part = pl.ds(start, size)
                got[name, c, start] = send(block.at[0, part], block.at[c, part], dev(dx=c))

    def across(name):
        block = blocks[name][1]
        got[name, 2, 0].wait_recv()
        for k in (4, 3, 5, 2, 6, 1, 7):
            got[name, 2, k] = send(block.at[2, 0], block.at[2, k], dev(dz=k))

    def arrive(c, name):
        for k in range(1, NZ) if c == 2 else (0, 1, 6, 3):
            got[name, c, k].wait_recv()

    def products(c, g):
        if c:
            for name in sorted({"g" if q == 2 else "x" for q in GROUPS[c][g]}):
                arrive(c, name)
        for i, q in enumerate(GROUPS[c][g]):
            left = (gb if q == 2 else xb)[c].reshape(NZ * t, w)
            for h in (1, 0):
                if q == 2:
                    part = dot_nt(left, buf["wd"][h])
                else:
                    part = dot(left, buf["wu" if q else "wg"][h])
                to = buf[f"{'cs' if h else 'po'}{c}{g}"]
                to[:, i] = part.reshape(NZ, t, f)
        got["c", c, g] = send(buf[f"cs{c}{g}"], buf[f"cr{c}{g}"], dev(other=True))

    def own(c, g, slot):
        return buf[f"po{c}{g}"][slot] + buf[f"cr{c}{g}"][slot]

    def leaf(c, g):
        got["c", c, g].wait_recv()
        pb, rr, ro = buf[f"pb{c}{g}"], buf[f"rr{c}{g}"], buf[f"ro{c}{g}"]
        for slot in range(NZ):
            pb[slot] = own(c, g, slot).astype(BF)
        got["l", c, g] = [
            send(pb.at[at_y(-3)], rr.at[0], y_dev(-1)),
            send(pb.at[at_y(-4)], rr.at[1], y_dev(-2)),
            send(pb.at[at_y(3)], rr.at[2], y_dev(1)),
        ]
        got["d", c, g] = [send(pb.at[at_y(-1)], ro.at[0], y_dev(-1)), send(pb.at[at_y(1)], ro.at[1], y_dev(1))]

    def relay(c, g):
        for copy in got["l", c, g]:
            copy.wait_recv()
        rr, sr, ro = buf[f"rr{c}{g}"], buf[f"sr{c}{g}"], buf[f"ro{c}{g}"]
        sr[0] = (own(c, g, at_y(-2)) + rr[0].astype(F32) + rr[1].astype(F32)).astype(BF)
        one = send(sr.at[0], ro.at[2], y_dev(-2))
        sr[1] = (own(c, g, at_y(2)) + rr[2].astype(F32)).astype(BF)
        got["d", c, g] += [one, send(sr.at[1], ro.at[3], y_dev(2))]

    def owner(c):
        sums = {}
        for g, qs in enumerate(GROUPS[c]):
            for copy in got["d", c, g]:
                copy.wait_recv()
            total = own(c, g, y)
            for i in range(4):
                total = total + buf[f"ro{c}{g}"][i].astype(F32)
            for i, q in enumerate(qs):
                sums[q] = total[i]
        gate, up, back = sums[0], sums[1], sums[2]
        sig = jax.nn.sigmoid(gate)
        silu = gate * sig
        hb[0, c, y, 0] = (back * up * sig * (1.0 + gate * (1.0 - sig))).astype(BF)
        hb[0, c, y, 1] = (back * silu).astype(BF)
        hh[0, y, c] = (silu * up).astype(BF)

    def result(c, slot):
        return hh.at[0, slot] if c == "h" else hb.at[0, c, slot]

    def spread(c):
        mine = result(c, y)
        for k in (2, -2, 1, -1):
            got["a", c, k] = send(mine, mine, y_dev(k))

    def pass_on(c):
        got["a", c, 2].wait_recv()
        block = result(c, at_y(-2))
        got["a", c, 4] = send(block, block, y_dev(2))
        got["a", c, 3] = send(block, block, y_dev(1))
        got["a", c, -2].wait_recv()
        block = result(c, at_y(2))
        got["a", c, -3] = send(block, block, y_dev(-1))

    def share(c):
        for k in (1, -1, 3, -3, 4):
            got["a", c, k].wait_recv()
        if c == "h":
            got["s", c] = send(hh.at[0], hh.at[1], dev(other=True))
        else:
            got["s", c] = send(hb.at[0, c], hb.at[1, c], dev(other=True))

    def back_product(c):
        got["s", c].wait_recv()
        total = None
        for h in range(2):
            for q, name in enumerate(("wg", "wu")):
                term = dot_nt(hb[h, c, :, q].reshape(NZ * t, f), buf[name][h])
                total = term if total is None else total + term
        total = total.reshape(NZ, t, w)
        if c in (1, 3):
            buf["xs"][c] = total.astype(BF)
            for start, size in PARTS:
                part = pl.ds(start, size)
                got["xq", c, start] = send(buf["xs"].at[c, part], buf["xq"].at[c, part], dev(dx=-c))
        elif c == 0:
            buf["d0"][...] = total
        else:
            to_z(c, lambda k: total[k], (4, 3, 5, 2, 6, 1, 7))

    def to_z(c, block, order):
        zs, zr = buf["zs"], buf["zr"]
        for k in order:
            zs[c, k] = block(k).astype(BF)
            got["zr", c, k] = send(zs.at[c, k], zr.at[c, k], dev(dz=-k))
        if 1 in order:
            buf["dx"][c] = block(0)

    def mix(far):
        for c in (1, 3):
            for start, _ in PARTS[:1] if far else PARTS[1:]:
                got["xq", c, start].wait_recv()
        xq = buf["xq"]
        order = (4, 3, 5) if far else (2, 6, 1, 7)
        to_z(0, lambda k: buf["d0"][k] + xq[1, k].astype(F32) + xq[3, k].astype(F32), order)

    def over_z(c):
        total = buf["dx"][c]
        for k in range(1, NZ):
            got["zr", c, k].wait_recv()
            total = total + buf["zr"][c, k].astype(F32)
        return total

    def over_x(c):
        buf["dx"][c] = over_z(c)
        got["xr", c] = send(buf["dx"].at[c], buf["xr"].at[c], dev(dx=-c))

    def weight_grads():
        left = xb[...].reshape(NX * NZ * t, w)
        for h in range(2):
            for q, out in ((0, og_ref), (1, ou_ref)):
                right = hb[h, :, :, q].reshape(NX * NZ * t, f)
                out[:, halves[h]] = dot_tn(left, right).astype(BF)

    def down_grad():
        right = gb[...].reshape(NX * NZ * t, w)
        got["s", "h"].wait_recv()
        for h in range(2):
            left = jnp.concatenate([hh[h, :, c].reshape(NY * t, f) for c in range(NX)], axis=0)
            od_ref[halves[h], :] = dot_tn(left, right).astype(BF)

    def finish():
        total = over_z(0)
        got["xr", 2].wait_recv()
        total = total + buf["xr"][2]
        dx_ref[...] = total.astype(BF)

    def settle():
        while started:
            started.pop().wait_send()

    first("x", 2)
    first("g", 2)
    column("x")
    first("x", 1)
    first("x", 3)
    column("g")
    first("g", 1)
    first("g", 3)
    for copy in loads:
        copy.wait()
    forward("x", False)
    forward("x", True)
    products(0, 0)
    across("x")
    leaf(0, 0)
    forward("g", False)
    forward("g", True)
    across("g")
    products(0, 1)
    products(1, 0)
    leaf(0, 1)
    relay(0, 0)
    products(3, 0)
    leaf(1, 0)
    leaf(3, 0)
    products(1, 1)
    products(3, 1)
    products(2, 0)
    relay(0, 1)
    leaf(1, 1)
    leaf(3, 1)
    products(2, 1)
    leaf(2, 0)
    leaf(2, 1)
    relay(1, 0)
    relay(1, 1)
    owner(0)
    relay(3, 0)
    relay(3, 1)
    relay(2, 0)
    relay(2, 1)
    spread(0)
    owner(1)
    spread(1)
    owner(3)
    spread(3)
    owner(2)
    spread(2)
    pass_on(1)
    pass_on(3)
    pass_on(2)
    pass_on(0)
    share(1)
    back_product(1)
    share(3)
    spread("h")
    share(2)
    back_product(3)
    back_product(2)
    share(0)
    pass_on("h")
    back_product(0)
    mix(True)
    mix(False)
    over_x(2)
    share("h")
    weight_grads()
    down_grad()
    settle()
    finish()


def copies(*refs):
    n, sem = len(refs) // 2, refs[-1]
    started = [pltpu.make_async_copy(refs[i], refs[n + i], sem.at[i]) for i in range(n)]
    for copy in started:
        copy.start()
    for copy in started:
        copy.wait()


def per_device(inputs, out_grad, gate_weight, up_weight, down_weight):
    t, w = inputs.shape
    f = gate_weight.shape[1] // 2
    buffers = scratch(t, w, f)
    vmem, hbm = pl.BlockSpec(memory_space=pltpu.VMEM), pl.BlockSpec(memory_space=pl.ANY)
    flops = 2 * 8 * (NX * NZ * t) * w * (2 * f)
    made = pl.pallas_call(
        functools.partial(kernel, list(buffers)),
        out_shape=(
            pltpu.VMEM(inputs.shape, BF),
            pltpu.VMEM(gate_weight.shape, BF),
            pltpu.VMEM(up_weight.shape, BF),
            pltpu.VMEM(down_weight.shape, BF),
        ),
        in_specs=[vmem, vmem, hbm, hbm, hbm],
        out_specs=(vmem,) * 4,
        scratch_shapes=[pltpu.VMEM(shape, dtype) for shape, dtype in buffers.values()]
        + [
            pltpu.SemaphoreType.DMA((N_REMOTE,)),
            pltpu.SemaphoreType.DMA((N_REMOTE,)),
            pltpu.SemaphoreType.DMA((N_LOCAL,)),
        ],
        compiler_params=pltpu.CompilerParams(collective_id=0, has_side_effects=True, vmem_limit_bytes=56 << 20),
        cost_estimate=pl.CostEstimate(flops=flops, bytes_accessed=4 << 20, transcendentals=3 * NX * t * f),
    )(inputs, out_grad, gate_weight, up_weight, down_weight)
    return pl.pallas_call(
        copies,
        out_shape=tuple(jax.ShapeDtypeStruct(a.shape, a.dtype) for a in made),
        in_specs=[vmem] * 4,
        out_specs=(hbm,) * 4,
        scratch_shapes=[pltpu.SemaphoreType.DMA((4,))],
        cost_estimate=pl.CostEstimate(flops=0, bytes_accessed=4 << 20, transcendentals=0),
    )(*(pltpu.with_memory_space_constraint(a, pltpu.VMEM) for a in made))

def solution(mesh):
    in_specs = (
        P("row", ("inw", "outw")),
        P("row", ("inw", "outw")),
        P(("inw", "outw"), "row"),
        P(("inw", "outw"), "row"),
        P("row", ("inw", "outw")),
    )
    out_specs = (
        P("row", ("inw", "outw")),
        P(("inw", "outw"), "row"),
        P(("inw", "outw"), "row"),
        P("row", ("inw", "outw")),
    )
    return jax.shard_map(per_device, mesh=mesh, in_specs=in_specs, out_specs=out_specs, check_vma=False)
```
